512 devices in a mesh: row: 32 (over y, x, core), col: 16 (over z).
Axes of the slice: x: 4, y: 4, z: 16, core: 2. Of those that a mesh axis runs over, the one named last changes fastest.
Arguments:
- features: bfloat16 [131072, 128], P('row'), may hold values from -4 to 4
- factor_prev: bfloat16 [131072, 2048], P('row', 'col'), may hold values from -0.125 to 0.125
- panel_index: int32 [1], replicated, may hold values from 0 to 511
Outputs:
- panel: float32 [131072, 256], P(('row', 'col'))
- log_det: float32 [1], replicated
The draws below stay inside these ranges and needn't reach their ends.
All inputs are finite; a program needn't handle non-finite values.
Results may differ from the reference program's by a relative error of at most 0.0003.
Values may be sent and summed in bfloat16 or wider, within the bound.
No kernel may reach another device: no remote copies, remote signals or barrier semaphores. Data moves between devices by JAX's collectives and lax.ppermute only.
A program may use at most 64 MiB of HBM per device.

```python
import jax
import jax.numpy as jnp
from jax import lax

FEAT = 128
TILE = 256
KPREV = 2048
ROWS_DEV = 4096
TILES = 512
ROWS = 131072
N_ROW = 32


def draw_features(key, part):
    key = jax.random.fold_in(key, 3)
    scale_key, value_key = jax.random.split(key)
    log_scale = jax.random.uniform(scale_key, (ROWS, 1), jnp.float32, jnp.log(0.25), 0.0)
    values = jnp.clip(jax.random.normal(value_key, (ROWS, FEAT), jnp.float32), -4.0, 4.0)
    return (jnp.exp(log_scale) * values).astype(jnp.bfloat16)


def level_of(stream_key, extent, pieces, smallest, high):
    gain = 1.0
    for dim, blocks in pieces:
        draws = jax.random.uniform(jax.random.fold_in(jax.random.fold_in(stream_key, 6), dim), (blocks,), jnp.float32, smallest / len(pieces), high / len(pieces))
        gain = gain * jnp.repeat(jnp.exp(draws), extent[dim] // blocks).reshape((-1,) + (1,) * (len(extent) - 1 - dim))
    return gain


def scatter_about(own_key, shape, width, bound, pieces=(), held_as=jnp.bfloat16):
    gain = level_of(own_key, shape, pieces, -0.22, 0.18) if pieces else 1.0
    array = jax.random.normal(own_key, shape, jnp.float32) * width * gain
    return jnp.minimum(jnp.maximum(array, -bound), bound).astype(held_as)


def setup_inputs(seed: int = 0) -> dict:
    splits = jax.random.split(jax.random.key(seed), 4)
    return {
        "features": draw_features(jax.random.fold_in(splits[3], 71), 0),
        "factor_prev": scatter_about(splits[1], (ROWS, KPREV), KPREV ** -0.5, 0.125, ((0, 32), (1, 16))),
        "panel_index": jax.random.randint(splits[2], (1,), 0, TILES).astype(jnp.int32),
    }


NUGGET = 4.0
RANGE = 8.0

def kernel_block(row_feat, panel_feat, self_pair):
    row_wide = row_feat.astype(jnp.float32)
    panel_wide = panel_feat.astype(jnp.float32)
    row_square = lax.optimization_barrier(jnp.sum(row_wide * row_wide, axis=1, keepdims=True))
    panel_square = lax.optimization_barrier(jnp.sum(panel_wide * panel_wide, axis=1))[None, :]
    cross_term = jnp.dot(row_feat.astype(jnp.float32), panel_feat.T.astype(jnp.float32), preferred_element_type=jnp.float32)
    squared = jnp.maximum(row_square + panel_square - 2.0 * cross_term, 0.0)
    distance = jnp.where(self_pair, jnp.float32(0.0), jnp.sqrt(squared))
    return jnp.exp(-distance / RANGE) + jnp.where(self_pair, jnp.float32(NUGGET), jnp.float32(0.0))

def reference(features, factor_prev, panel_index):
    panel_tile = panel_index[0].astype(jnp.int32)
    owner_row = panel_tile % N_ROW
    local_tile = panel_tile // N_ROW
    begin_row = (owner_row * ROWS_DEV + local_tile * TILE).astype(jnp.int32)
    panel_feat = lax.dynamic_slice_in_dim(features, begin_row, TILE, 0)
    panel_fac = lax.dynamic_slice_in_dim(factor_prev, begin_row, TILE, 0)
    row_index = jnp.arange(ROWS, dtype=jnp.int32)
    tile_of = row_index % ROWS_DEV // TILE * N_ROW + row_index // ROWS_DEV
    offset = row_index % TILE
    self_pair = (tile_of == panel_tile)[:, None] & (offset[:, None] == jnp.arange(TILE, dtype=jnp.int32)[None, :])
    kernel = kernel_block(features, panel_feat, self_pair)
    update = jnp.dot(factor_prev.astype(jnp.float32), panel_fac.T.astype(jnp.float32), preferred_element_type=jnp.float32)
    column_block = kernel - update
    diagonal = lax.dynamic_slice_in_dim(column_block, begin_row, TILE, 0)
    diagonal_factor = jnp.linalg.cholesky(diagonal)
    identity = jnp.eye(TILE, dtype=jnp.float32)
    inverse = lax.linalg.triangular_solve(diagonal_factor, identity, left_side=True, lower=True)
    panel = jnp.dot(column_block, inverse.T, precision=lax.Precision.HIGHEST)
    panel = jnp.where((tile_of >= panel_tile)[:, None], panel, jnp.float32(0.0))
    log_det = 2.0 * jnp.sum(jnp.log(jnp.diagonal(diagonal_factor))) / TILE
    return (panel, jnp.reshape(log_det, (1,)))
```

```python
import jax
import jax.numpy as jnp
from jax import lax
from jax.sharding import PartitionSpec as P

TILE = 256
NUGGET = 4.0
RANGE = 8.0
CHUNKS = 8
PIECE = TILE // CHUNKS
FEAT_PIECE = 8
SLOT = PIECE + FEAT_PIECE


def kernel_block(row_feat, panel_feat, self_pair):
    row_wide = row_feat.astype(jnp.float32)
    panel_wide = panel_feat.astype(jnp.float32)
    row_square = jnp.sum(row_wide * row_wide, axis=1, keepdims=True)
    panel_square = jnp.sum(panel_wide * panel_wide, axis=1)[None, :]
    cross_term = jnp.dot(row_feat, panel_feat.T, preferred_element_type=jnp.float32)
    squared = jnp.maximum(row_square + panel_square - 2.0 * cross_term, 0.0)
    distance = jnp.where(self_pair, jnp.float32(0.0), jnp.sqrt(squared))
    return jnp.exp(-distance / RANGE) + jnp.where(self_pair, jnp.float32(NUGGET), jnp.float32(0.0))


def gather_panel(own_fac, own_feat, owner_row):
    width = own_fac.shape[1]
    col_count = lax.axis_size("col")
    my_col = lax.axis_index("col")
    fac_chunks = own_fac.reshape(CHUNKS, PIECE, width)
    feat_chunks = own_feat.reshape(CHUNKS, 4, FEAT_PIECE, width)
    feat_chunks = lax.dynamic_index_in_dim(feat_chunks, my_col % 4, 1, keepdims=False)
    slots = jnp.concatenate([fac_chunks, feat_chunks], axis=1)
    send = jnp.concatenate([slots] * 4, axis=0)
    got = lax.all_to_all(send, "row", 0, 0, tiled=True)
    slot = lax.dynamic_index_in_dim(got, owner_row, 0, keepdims=True)
    layers = lax.all_to_all(jnp.broadcast_to(slot, (col_count, SLOT, width)), "col", 0, 0, tiled=True)
    over_x = [[(y * 4 + x) * 2 + c for x in range(4)] for y in range(4) for c in range(2)]
    copies = jnp.broadcast_to(layers[None], (4, col_count, SLOT, width))
    mine = lax.all_to_all(copies, "row", 0, 0, tiled=True, axis_index_groups=over_x)
    other = lax.ppermute(mine, "row", [(i, i ^ 1) for i in range(32)])
    first = lax.axis_index("row") % 2 == 0
    both = jnp.stack([jnp.where(first, mine, other), jnp.where(first, other, mine)], axis=1)
    fac = both[:, :, :, :PIECE].transpose(0, 1, 3, 2, 4).reshape(TILE, col_count * width)
    feat = both[:, :, :4, PIECE:].reshape(TILE, width)
    return fac, feat


def body(features, factor_prev, panel_index):
    row_count = lax.axis_size("row")
    col_count = lax.axis_size("col")
    my_rows = features.shape[0] // col_count
    width = factor_prev.shape[1]
    panel_tile = panel_index[0]
    owner_row = panel_tile % row_count
    local_tile = panel_tile // row_count
    my_col = lax.axis_index("col")
    my_row = lax.axis_index("row")
    my_fac = lax.all_to_all(factor_prev.reshape(col_count, my_rows, width), "col", 0, 0, tiled=True)
    own_feat = lax.dynamic_slice_in_dim(features, local_tile * TILE, TILE, 0)
    own_fac = lax.dynamic_slice_in_dim(factor_prev, local_tile * TILE, TILE, 0)
    panel_fac, panel_feat = gather_panel(own_fac, own_feat, owner_row)
    columns = jnp.arange(TILE, dtype=jnp.int32)
    identity_mask = columns[:, None] == columns[None, :]
    diagonal_update = jnp.dot(panel_fac, panel_fac.T, preferred_element_type=jnp.float32)
    diagonal = kernel_block(panel_feat, panel_feat, identity_mask) - diagonal_update
    diagonal_factor = jnp.linalg.cholesky(diagonal)
    identity = jnp.eye(TILE, dtype=jnp.float32)
    inverse = lax.linalg.triangular_solve(diagonal_factor, identity, left_side=True, lower=True)
    my_feat = lax.dynamic_slice_in_dim(features, my_col * my_rows, my_rows, 0)
    tile_of = my_col * row_count + my_row
    self_pair = (tile_of == panel_tile) & identity_mask
    my_fac = my_fac.transpose(1, 0, 2).reshape(my_rows, col_count * width)
    update = jnp.dot(my_fac, panel_fac.T, preferred_element_type=jnp.float32)
    column_block = kernel_block(my_feat, panel_feat, self_pair) - update
    panel = jnp.dot(column_block, inverse.T, precision=lax.Precision.HIGHEST)
    panel = jnp.where(tile_of >= panel_tile, panel, jnp.float32(0.0))
    log_det = 2.0 * jnp.sum(jnp.log(jnp.diagonal(diagonal_factor))) / TILE
    return (panel, jnp.reshape(log_det, (1,)))


def solution(mesh):
    in_specs = (P("row", None), P("row", "col"), P())
    out_specs = (P(("row", "col"), None), P())
    return jax.shard_map(body, mesh=mesh, in_specs=in_specs, out_specs=out_specs, check_vma=False)
```

```python
import jax
import jax.numpy as jnp
from jax import lax
from jax.experimental import pallas as pl
from jax.experimental.pallas import tpu as pltpu
from jax.sharding import PartitionSpec as P

TILE = 256
FEAT = 128
NUGGET = 4.0
RANGE = 8.0
CHUNKS = 8
PIECE = TILE // CHUNKS
FEAT_PIECE = 8
BLOCK = 32
SUB = 8
LANES = 128
VMEM_LIMIT = 40 * 2**20


def tile_kernel(row_feat, panel_feat, self_pair):
    row_wide = row_feat.astype(jnp.float32)
    panel_wide = panel_feat.astype(jnp.float32)
    row_square = jnp.sum(row_wide * row_wide, axis=1, keepdims=True)
    square = panel_wide * panel_wide
    high = square.astype(jnp.bfloat16)
    low = (square - high.astype(jnp.float32)).astype(jnp.bfloat16)
    ones = jnp.ones((SUB, panel_feat.shape[1]), jnp.bfloat16)
    panel_square = (dot_last(ones, high) + dot_last(ones, low))[:1, :]
    cross_term = dot_last(row_feat, panel_feat)
    squared = jnp.maximum(row_square + panel_square - 2.0 * cross_term, 0.0)
    distance = jnp.where(self_pair, 0.0, jnp.sqrt(squared))
    return jnp.exp(-distance / RANGE) + jnp.where(self_pair, NUGGET, 0.0)


def dot_last(a, b):
    return lax.dot_general(a, b, (((1,), (1,)), ((), ())), preferred_element_type=jnp.float32)


def split3(a):
    high = a.astype(jnp.bfloat16)
    rest = a - high.astype(jnp.float32)
    mid = rest.astype(jnp.bfloat16)
    low = (rest - mid.astype(jnp.float32)).astype(jnp.bfloat16)
    return high, mid, low


def factor_rows(work, inverse, block, pivots, sub, lane, lane_wide):
    count = BLOCK // SUB
    begin = block * BLOCK
    base = begin // LANES * LANES
    diag, rows = [], []
    for i in range(count):
        row = work[begin + i * SUB : begin + (i + 1) * SUB, :]
        diag.append(row[:, base : base + LANES])
        inside = (lane_wide >= begin) & (lane_wide < begin + BLOCK)
        eye = lane_wide == begin + i * SUB + lax.broadcasted_iota(jnp.int32, (SUB, TILE), 0)
        rows.append(jnp.where(inside, eye.astype(jnp.float32), row))
    for j in range(count):
        first = begin - base + j * SUB
        column = [
            [jnp.broadcast_to(diag[i][:, first + k : first + k + 1], (SUB, LANES)) for k in range(SUB)]
            for i in range(j, count)
        ]
        pivot = jnp.ones((SUB, LANES), jnp.float32)
        for k in range(SUB):
            value = jnp.broadcast_to(column[0][k][k : k + 1, :], (SUB, LANES))
            recip = 1.0 / value
            pivot = jnp.where(sub == k, value, pivot)
            factor = [c[k] * recip for c in column]
            factor[0] = jnp.where(sub > k, factor[0], 0.0)
            for m in range(k + 1, SUB):
                other = jnp.broadcast_to(column[0][k][m : m + 1, :], (SUB, LANES))
                for i in range(len(column)):
                    column[i][m] = column[i][m] - factor[i] * other
            row_k = jnp.broadcast_to(rows[j][k : k + 1, :], (SUB, TILE))
            diag_k = jnp.broadcast_to(diag[j][k : k + 1, :], (SUB, LANES))
            for i in range(len(column)):
                rows[j + i] = rows[j + i] - jnp.concatenate([factor[i], factor[i]], axis=1) * row_k
                diag[j + i] = diag[j + i] - factor[i] * diag_k
        scale = 1.0 / jnp.sqrt(pivot)
        pivots = jnp.where(lane == block * count + j, pivot, pivots)
        rows[j] = rows[j] * jnp.concatenate([scale, scale], axis=1)
    whole = jnp.concatenate(rows, axis=0)
    inverse[begin : begin + BLOCK, :] = jnp.where(lane_wide < begin + BLOCK, whole, 0.0)
    return whole, pivots


def factor_tile(work, inverse):
    sub = lax.broadcasted_iota(jnp.int32, (SUB, LANES), 0)
    lane = lax.broadcasted_iota(jnp.int32, (SUB, LANES), 1)
    lane_wide = lax.broadcasted_iota(jnp.int32, (1, TILE), 1)
    pivots = jnp.ones((SUB, LANES), jnp.float32)
    for block in range(TILE // BLOCK):
        whole, pivots = factor_rows(work, inverse, block, pivots, sub, lane, lane_wide)
        end = (block + 1) * BLOCK
        if end == TILE:
            break
        base = end // LANES * LANES
        high, mid, low = split3(whole)
        left = jnp.concatenate([p[:, base:] for p in (high, high, mid, high, low, mid)], axis=0)
        right = jnp.concatenate([high, mid, high, low, high, mid], axis=0)
        update = lax.dot_general(left, right, (((0,), (0,)), ((), ())), preferred_element_type=jnp.float32)
        old = jnp.where((lane_wide >= end - BLOCK) & (lane_wide < end), 0.0, work[end:, :])
        work[end:, :] = old - update[end - base :, :]
    return jnp.sum(jnp.log(pivots)) / TILE


def diagonal_kernel(core, mine, other, inverse, log_det, panel_fac, panel_feat, work):
    layers = panel_fac.shape[1] // LANES
    for c in range(2):

        def place(source, c=c):
            for x in range(CHUNKS // 2):
                begin = (x * 2 + c) * PIECE
                for z in range(layers):
                    panel_fac[begin : begin + PIECE, z * LANES : (z + 1) * LANES] = source[
                        x, z * PIECE : (z + 1) * PIECE, :
                    ]
                panel_feat[begin : begin + PIECE, :] = source[x, layers * PIECE :, :]

        pl.when(core[0] == c)(lambda: place(mine))
        pl.when(core[0] != c)(lambda: place(other))
    row = lax.broadcasted_iota(jnp.int32, (TILE, TILE), 0)
    col = lax.broadcasted_iota(jnp.int32, (TILE, TILE), 1)
    feat = panel_feat[...]
    fac = panel_fac[...]
    work[...] = tile_kernel(feat, feat, row == col) - dot_last(fac, fac)
    log_det[...] = jnp.full((1, LANES), factor_tile(work, inverse), jnp.float32)


def panel_kernel(where, feat, fac, panel_feat, panel_fac, inverse, panel):
    tile_of = where[1]
    panel_tile = where[2]
    row = lax.broadcasted_iota(jnp.int32, (TILE, TILE), 0)
    col = lax.broadcasted_iota(jnp.int32, (TILE, TILE), 1)
    self_pair = (row == col) & (tile_of == panel_tile)
    rows = jnp.concatenate([fac[z] for z in range(fac.shape[0])], axis=1)
    update = dot_last(rows, panel_fac[...])
    block = tile_kernel(feat[...], panel_feat[...], self_pair) - update
    result = lax.dot_general(
        block,
        inverse[...],
        (((1,), (1,)), ((), ())),
        precision=lax.Precision.HIGHEST,
        preferred_element_type=jnp.float32,
    )
    panel[...] = jnp.where(tile_of >= panel_tile, result, 0.0)


def gather_panel(own_fac, own_feat, owner_row):
    width = own_fac.shape[1]
    col_count = lax.axis_size("col")
    my_col = lax.axis_index("col")
    fac_chunks = own_fac.reshape(CHUNKS, PIECE, width)
    feat_chunks = own_feat.reshape(CHUNKS, 4, FEAT_PIECE, width)
    feat_chunks = lax.dynamic_index_in_dim(feat_chunks, my_col % 4, 1, keepdims=False)
    slots = jnp.concatenate([fac_chunks, feat_chunks], axis=1)
    send = jnp.concatenate([slots] * 4, axis=0)
    got = lax.all_to_all(send, "row", 0, 0, tiled=True)
    slot = lax.dynamic_index_in_dim(got, owner_row, 0, keepdims=True)
    layers = lax.all_to_all(jnp.broadcast_to(slot, (col_count,) + slot.shape[1:]), "col", 0, 0, tiled=True)
    over_x = [[(y * 4 + x) * 2 + c for x in range(4)] for y in range(4) for c in range(2)]
    chunk = jnp.concatenate(
        [layers[:, :PIECE].reshape(col_count * PIECE, width), layers[:4, PIECE:].reshape(PIECE, width)], axis=0
    )
    copies = jnp.broadcast_to(chunk[None], (4,) + chunk.shape)
    mine = lax.all_to_all(copies, "row", 0, 0, tiled=True, axis_index_groups=over_x)
    other = lax.ppermute(mine, "row", [(i, i ^ 1) for i in range(32)])
    return mine, other


def body(features, factor_prev, panel_index):
    row_count = lax.axis_size("row")
    col_count = lax.axis_size("col")
    my_rows = features.shape[0] // col_count
    width = factor_prev.shape[1]
    panel_tile = panel_index[0]
    owner_row = panel_tile % row_count
    local_tile = panel_tile // row_count
    my_col = lax.axis_index("col")
    my_row = lax.axis_index("row")
    my_fac = lax.all_to_all(factor_prev.reshape(col_count, my_rows, width), "col", 0, 0, tiled=True)
    own_feat = lax.dynamic_slice_in_dim(features, local_tile * TILE, TILE, 0)
    own_fac = lax.dynamic_slice_in_dim(factor_prev, local_tile * TILE, TILE, 0)
    mine, other = gather_panel(own_fac, own_feat, owner_row)
    vmem = pl.BlockSpec(memory_space=pltpu.VMEM)
    smem = pl.BlockSpec(memory_space=pltpu.SMEM)
    inverse, log_det, panel_fac, panel_feat = pl.pallas_call(
        diagonal_kernel,
        out_shape=(
            jax.ShapeDtypeStruct((TILE, TILE), jnp.float32),
            jax.ShapeDtypeStruct((1, LANES), jnp.float32),
            jax.ShapeDtypeStruct((TILE, col_count * width), jnp.bfloat16),
            jax.ShapeDtypeStruct((TILE, FEAT), jnp.bfloat16),
        ),
        in_specs=[smem, vmem, vmem],
        out_specs=(vmem, vmem, vmem, vmem),
        scratch_shapes=[pltpu.VMEM((TILE, TILE), jnp.float32)],
        compiler_params=pltpu.CompilerParams(vmem_limit_bytes=VMEM_LIMIT),
        cost_estimate=pl.CostEstimate(flops=10**10, bytes_accessed=4 * 10**6, transcendentals=10**5),
    )((my_row % 2).reshape(1), mine, other)
    tile_of = my_col * row_count + my_row
    where = jnp.stack([my_col, tile_of, panel_tile]).astype(jnp.int32)
    whole = lambda *shape: pl.BlockSpec(shape, lambda i, where: (0,) * len(shape))
    panel = pl.pallas_call(
        panel_kernel,
        out_shape=jax.ShapeDtypeStruct((TILE, TILE), jnp.float32),
        grid_spec=pltpu.PrefetchScalarGridSpec(
            num_scalar_prefetch=1,
            grid=(1,),
            in_specs=[
                pl.BlockSpec((TILE, FEAT), lambda i, where: (where[0], 0)),
                whole(col_count, my_rows, width),
                whole(TILE, FEAT),
                whole(TILE, col_count * width),
                whole(TILE, TILE),
            ],
            out_specs=whole(TILE, TILE),
        ),
        compiler_params=pltpu.CompilerParams(vmem_limit_bytes=VMEM_LIMIT),
        cost_estimate=pl.CostEstimate(flops=10**9, bytes_accessed=4 * 10**6, transcendentals=10**5),
    )(where, features, my_fac, panel_feat, panel_fac, inverse)
    return (panel, log_det[0, :1])


def solution(mesh):
    in_specs = (P("row", None), P("row", "col"), P())
    out_specs = (P(("row", "col"), None), P())
    return jax.shard_map(body, mesh=mesh, in_specs=in_specs, out_specs=out_specs, check_vma=False)
```

```python
import jax
import jax.numpy as jnp
import numpy as np
from jax import lax
from jax.experimental import pallas as pl
from jax.experimental.pallas import tpu as pltpu
from jax.sharding import PartitionSpec as P

TILE = 256
FEAT = 128
NUGGET = 4.0
RANGE = 8.0
CHUNKS = 32
PIECE = TILE // CHUNKS
BLOCK = 32
SUB = 8
LANES = 128
VMEM_LIMIT = 40 * 2**20


def tile_kernel(row_feat, panel_feat, self_pair):
    row_wide = row_feat.astype(jnp.float32)
    panel_wide = panel_feat.astype(jnp.float32)
    row_square = jnp.sum(row_wide * row_wide, axis=1, keepdims=True)
    square = panel_wide * panel_wide
    high = square.astype(jnp.bfloat16)
    low = (square - high.astype(jnp.float32)).astype(jnp.bfloat16)
    ones = jnp.ones((SUB, panel_feat.shape[1]), jnp.bfloat16)
    panel_square = (dot_last(ones, high) + dot_last(ones, low))[:1, :]
    cross_term = dot_last(row_feat, panel_feat)
    squared = jnp.maximum(row_square + panel_square - 2.0 * cross_term, 0.0)
    distance = jnp.where(self_pair, 0.0, jnp.sqrt(squared))
    return jnp.exp(-distance / RANGE) + jnp.where(self_pair, NUGGET, 0.0)


def dot_last(a, b):
    return lax.dot_general(a, b, (((1,), (1,)), ((), ())), preferred_element_type=jnp.float32)


def split3(a):
    high = a.astype(jnp.bfloat16)
    rest = a - high.astype(jnp.float32)
    mid = rest.astype(jnp.bfloat16)
    low = (rest - mid.astype(jnp.float32)).astype(jnp.bfloat16)
    return high, mid, low


def factor_rows(work, inverse, block, pivots, sub, lane, lane_wide):
    count = BLOCK // SUB
    begin = block * BLOCK
    base = begin // LANES * LANES
    diag, rows = [], []
    for i in range(count):
        row = work[begin + i * SUB : begin + (i + 1) * SUB, :]
        diag.append(row[:, base : base + LANES])
        inside = (lane_wide >= begin) & (lane_wide < begin + BLOCK)
        eye = lane_wide == begin + i * SUB + lax.broadcasted_iota(jnp.int32, (SUB, TILE), 0)
        rows.append(jnp.where(inside, eye.astype(jnp.float32), row))
    for j in range(count):
        first = begin - base + j * SUB
        column = [
            [jnp.broadcast_to(diag[i][:, first + k : first + k + 1], (SUB, LANES)) for k in range(SUB)]
            for i in range(j, count)
        ]
        pivot = jnp.ones((SUB, LANES), jnp.float32)
        for k in range(SUB):
            value = jnp.broadcast_to(column[0][k][k : k + 1, :], (SUB, LANES))
            recip = 1.0 / value
            pivot = jnp.where(sub == k, value, pivot)
            factor = [c[k] * recip for c in column]
            factor[0] = jnp.where(sub > k, factor[0], 0.0)
            for m in range(k + 1, SUB):
                other = jnp.broadcast_to(column[0][k][m : m + 1, :], (SUB, LANES))
                for i in range(len(column)):
                    column[i][m] = column[i][m] - factor[i] * other
            row_k = jnp.broadcast_to(rows[j][k : k + 1, :], (SUB, TILE))
            diag_k = jnp.broadcast_to(diag[j][k : k + 1, :], (SUB, LANES))
            for i in range(len(column)):
                rows[j + i] = rows[j + i] - jnp.concatenate([factor[i], factor[i]], axis=1) * row_k
                diag[j + i] = diag[j + i] - factor[i] * diag_k
        scale = 1.0 / jnp.sqrt(pivot)
        pivots = jnp.where(lane == block * count + j, pivot, pivots)
        rows[j] = rows[j] * jnp.concatenate([scale, scale], axis=1)
    whole = jnp.concatenate(rows, axis=0)
    inverse[begin : begin + BLOCK, :] = jnp.where(lane_wide < begin + BLOCK, whole, 0.0)
    return whole, pivots


def factor_tile(work, inverse):
    sub = lax.broadcasted_iota(jnp.int32, (SUB, LANES), 0)
    lane = lax.broadcasted_iota(jnp.int32, (SUB, LANES), 1)
    lane_wide = lax.broadcasted_iota(jnp.int32, (1, TILE), 1)
    pivots = jnp.ones((SUB, LANES), jnp.float32)
    for block in range(TILE // BLOCK):
        whole, pivots = factor_rows(work, inverse, block, pivots, sub, lane, lane_wide)
        end = (block + 1) * BLOCK
        if end == TILE:
            break
        base = end // LANES * LANES
        high, mid, low = split3(whole)
        left = jnp.concatenate([p[:, base:] for p in (high, high, mid, high, low, mid)], axis=0)
        right = jnp.concatenate([high, mid, high, low, high, mid], axis=0)
        update = lax.dot_general(left, right, (((0,), (0,)), ((), ())), preferred_element_type=jnp.float32)
        old = jnp.where((lane_wide >= end - BLOCK) & (lane_wide < end), 0.0, work[end:, :])
        work[end:, :] = old - update[end - base :, :]
    return jnp.sum(jnp.log(pivots)) / TILE


def send_kernel(panel_index, features, factor_prev, send):
    fac = factor_prev[...].astype(jnp.float32).reshape(CHUNKS, PIECE, LANES)
    feat = features[...].astype(jnp.float32).reshape(CHUNKS, PIECE, LANES)
    send[...] = jnp.concatenate([fac, feat], axis=1).astype(jnp.bfloat16)


def diagonal_kernel(panel_fac, panel_feat, inverse, log_det, work):
    row = lax.broadcasted_iota(jnp.int32, (TILE, TILE), 0)
    col = lax.broadcasted_iota(jnp.int32, (TILE, TILE), 1)
    feat = panel_feat[...]
    fac = panel_fac[...]
    work[...] = tile_kernel(feat, feat, row == col) - dot_last(fac, fac)
    log_det[...] = jnp.full((1, LANES), factor_tile(work, inverse), jnp.float32)


def panel_kernel(where, feat, fac, panel_feat, panel_fac, inverse, panel):
    tile_of = where[1]
    panel_tile = where[2]
    row = lax.broadcasted_iota(jnp.int32, (TILE, TILE), 0)
    col = lax.broadcasted_iota(jnp.int32, (TILE, TILE), 1)
    self_pair = (row == col) & (tile_of == panel_tile)
    rows = jnp.concatenate([fac[z] for z in range(fac.shape[0])], axis=1)
    update = dot_last(rows, panel_fac[...])
    block = tile_kernel(feat[...], panel_feat[...], self_pair) - update
    result = lax.dot_general(
        block,
        inverse[...],
        (((1,), (1,)), ((), ())),
        precision=lax.Precision.HIGHEST,
        preferred_element_type=jnp.float32,
    )
    panel[...] = jnp.where(tile_of >= panel_tile, result, 0.0)


def groups_of(axis):
    index = np.arange(32).reshape(4, 4, 2)
    return np.moveaxis(index, {"y": 0, "x": 1}[axis], 2).reshape(-1, 4).tolist()


def gather_panel(send, owner_row):
    width = send.shape[2]
    col_count = lax.axis_size("col")
    got = lax.all_to_all(send, "row", 0, 0, tiled=True)
    slot = lax.dynamic_index_in_dim(got, owner_row, 0, keepdims=False)
    copies = jnp.broadcast_to(slot[None, :PIECE], (col_count, PIECE, width))
    layers = lax.all_to_all(copies, "col", 0, 0, tiled=True)
    return layers, slot[PIECE:]


def gather_chunks(layers, feat):
    col_count, _, width = layers.shape
    chunk = jnp.concatenate([layers.reshape(col_count * PIECE, width), feat], axis=0)
    over_x = lax.all_gather(chunk, "row", axis=0, axis_index_groups=groups_of("x"))
    mine = lax.all_gather(over_x, "row", axis=0, axis_index_groups=groups_of("y"))
    other = lax.ppermute(mine, "row", [(i, i ^ 1) for i in range(32)])
    first = lax.axis_index("row") % 2 == 0
    both = jnp.stack([jnp.where(first, mine, other), jnp.where(first, other, mine)], axis=2)
    fac = both[:, :, :, : col_count * PIECE].reshape(CHUNKS, col_count, PIECE, width)
    fac = fac.transpose(0, 2, 1, 3).reshape(TILE, col_count * width)
    return fac, both[:, :, :, col_count * PIECE :].reshape(TILE, width)


def body(features, factor_prev, panel_index):
    row_count = lax.axis_size("row")
    col_count = lax.axis_size("col")
    my_rows = features.shape[0] // col_count
    width = factor_prev.shape[1]
    panel_tile = panel_index[0]
    owner_row = panel_tile % row_count
    my_col = lax.axis_index("col")
    my_row = lax.axis_index("row")
    tiles = factor_prev.reshape(col_count, my_rows, width)
    tile_rows = pl.BlockSpec((TILE, LANES), lambda i, index: (lax.div(index[0], row_count), 0))
    send = pl.pallas_call(
        send_kernel,
        out_shape=jax.ShapeDtypeStruct((CHUNKS, 2 * PIECE, LANES), jnp.bfloat16),
        grid_spec=pltpu.PrefetchScalarGridSpec(
            num_scalar_prefetch=1,
            grid=(1,),
            in_specs=[tile_rows, tile_rows],
            out_specs=pl.BlockSpec((CHUNKS, 2 * PIECE, LANES), lambda i, index: (0, 0, 0)),
        ),
    )(panel_index, features, factor_prev)
    layers, feat_rows = gather_panel(send, owner_row)
    tiles, layers = lax.optimization_barrier((tiles, layers))
    my_fac = lax.all_to_all(tiles, "col", 0, 0, tiled=True)
    panel_fac, panel_feat = gather_chunks(layers, feat_rows)
    vmem = pl.BlockSpec(memory_space=pltpu.VMEM)
    inverse, log_det = pl.pallas_call(
        diagonal_kernel,
        out_shape=(
            jax.ShapeDtypeStruct((TILE, TILE), jnp.float32),
            jax.ShapeDtypeStruct((1, LANES), jnp.float32),
        ),
        in_specs=[vmem, vmem],
        out_specs=(vmem, vmem),
        scratch_shapes=[pltpu.VMEM((TILE, TILE), jnp.float32)],
        compiler_params=pltpu.CompilerParams(vmem_limit_bytes=VMEM_LIMIT),
        cost_estimate=pl.CostEstimate(flops=10**10, bytes_accessed=4 * 10**6, transcendentals=10**5),
    )(panel_fac, panel_feat)
    tile_of = my_col * row_count + my_row
    where = jnp.stack([my_col, tile_of, panel_tile]).astype(jnp.int32)
    whole = lambda *shape: pl.BlockSpec(shape, lambda i, where: (0,) * len(shape))
    panel = pl.pallas_call(
        panel_kernel,
        out_shape=jax.ShapeDtypeStruct((TILE, TILE), jnp.float32),
        grid_spec=pltpu.PrefetchScalarGridSpec(
            num_scalar_prefetch=1,
            grid=(1,),
            in_specs=[
                pl.BlockSpec((TILE, FEAT), lambda i, where: (where[0], 0)),
                whole(col_count, my_rows, width),
                whole(TILE, FEAT),
                whole(TILE, col_count * width),
                whole(TILE, TILE),
            ],
            out_specs=whole(TILE, TILE),
        ),
        compiler_params=pltpu.CompilerParams(vmem_limit_bytes=VMEM_LIMIT),
        cost_estimate=pl.CostEstimate(flops=10**9, bytes_accessed=4 * 10**6, transcendentals=10**5),
    )(where, features, my_fac, panel_feat, panel_fac, inverse)
    return (panel, log_det[0, :1])


def solution(mesh):
    in_specs = (P("row", None), P("row", "col"), P())
    out_specs = (P(("row", "col"), None), P())
    return jax.shard_map(body, mesh=mesh, in_specs=in_specs, out_specs=out_specs, check_vma=False)
```

```python
import jax
import jax.numpy as jnp
import numpy as np
from jax import lax
from jax.experimental import pallas as pl
from jax.experimental.pallas import tpu as pltpu
from jax.sharding import PartitionSpec as P

TILE = 256
FEAT = 128
NUGGET = 4.0
RANGE = 8.0
CHUNKS = 32
PIECE = TILE // CHUNKS
BLOCK = 32
SUB = 8
LANES = 128
VMEM_LIMIT = 40 * 2**20


def tile_kernel(row_feat, panel_feat, self_pair):
    row_wide = row_feat.astype(jnp.float32)
    panel_wide = panel_feat.astype(jnp.float32)
    row_square = jnp.sum(row_wide * row_wide, axis=1, keepdims=True)
    square = panel_wide * panel_wide
    high = square.astype(jnp.bfloat16)
    low = (square - high.astype(jnp.float32)).astype(jnp.bfloat16)
    ones = jnp.ones((SUB, panel_feat.shape[1]), jnp.bfloat16)
    panel_square = (dot_last(ones, high) + dot_last(ones, low))[:1, :]
    cross_term = dot_last(row_feat, panel_feat)
    squared = jnp.maximum(row_square + panel_square - 2.0 * cross_term, 0.0)
    distance = jnp.where(self_pair, 0.0, jnp.sqrt(squared))
    return jnp.exp(-distance / RANGE) + jnp.where(self_pair, NUGGET, 0.0)


def dot_last(a, b):
    return lax.dot_general(a, b, (((1,), (1,)), ((), ())), preferred_element_type=jnp.float32)


def split3(a):
    high = a.astype(jnp.bfloat16)
    rest = a - high.astype(jnp.float32)
    mid = rest.astype(jnp.bfloat16)
    low = (rest - mid.astype(jnp.float32)).astype(jnp.bfloat16)
    return high, mid, low


def factor_rows(work, inverse, block, pivots, sub, lane, lane_wide):
    count = BLOCK // SUB
    begin = block * BLOCK
    base = begin // LANES * LANES
    diag, rows = [], []
    for i in range(count):
        row = work[begin + i * SUB : begin + (i + 1) * SUB, :]
        diag.append(row[:, base : base + LANES])
        inside = (lane_wide >= begin) & (lane_wide < begin + BLOCK)
        eye = lane_wide == begin + i * SUB + lax.broadcasted_iota(jnp.int32, (SUB, TILE), 0)
        rows.append(jnp.where(inside, eye.astype(jnp.float32), row))

    def columns_of(j):
        first = begin - base + j * SUB
        return [
            [jnp.broadcast_to(diag[i][:, first + k : first + k + 1], (SUB, LANES)) for k in range(SUB)]
            for i in range(j, count)
        ]

    column = columns_of(0)
    for j in range(count):
        after = columns_of(j + 1) if j + 1 < count else []
        pivot = jnp.ones((SUB, LANES), jnp.float32)
        for k in range(SUB):
            value = jnp.broadcast_to(column[0][k][k : k + 1, :], (SUB, LANES))
            recip = 1.0 / value
            pivot = jnp.where(sub == k, value, pivot)
            factor = [c[k] * recip for c in column]
            factor[0] = jnp.where(sub > k, factor[0], 0.0)
            for m in range(k + 1, SUB):
                other = jnp.broadcast_to(column[0][k][m : m + 1, :], (SUB, LANES))
                for i in range(len(column)):
                    column[i][m] = column[i][m] - factor[i] * other
            for m in range(SUB if after else 0):
                other = jnp.broadcast_to(column[1][k][m : m + 1, :], (SUB, LANES))
                for i in range(len(after)):
                    after[i][m] = after[i][m] - factor[i + 1] * other
            row_k = jnp.broadcast_to(rows[j][k : k + 1, :], (SUB, TILE))
            diag_k = jnp.broadcast_to(diag[j][k : k + 1, :], (SUB, LANES))
            for i in range(len(column)):
                rows[j + i] = rows[j + i] - jnp.concatenate([factor[i], factor[i]], axis=1) * row_k
                diag[j + i] = diag[j + i] - factor[i] * diag_k
        scale = 1.0 / jnp.sqrt(pivot)
        pivots = jnp.where(lane == block * count + j, pivot, pivots)
        rows[j] = rows[j] * jnp.concatenate([scale, scale], axis=1)
        column = after
    whole = jnp.concatenate(rows, axis=0)
    inverse[begin : begin + BLOCK, :] = jnp.where(lane_wide < begin + BLOCK, whole, 0.0)
    return whole, pivots


def factor_tile(work, inverse):
    sub = lax.broadcasted_iota(jnp.int32, (SUB, LANES), 0)
    lane = lax.broadcasted_iota(jnp.int32, (SUB, LANES), 1)
    lane_wide = lax.broadcasted_iota(jnp.int32, (1, TILE), 1)
    pivots = jnp.ones((SUB, LANES), jnp.float32)
    for block in range(TILE // BLOCK):
        whole, pivots = factor_rows(work, inverse, block, pivots, sub, lane, lane_wide)
        end = (block + 1) * BLOCK
        if end == TILE:
            break
        base = end // LANES * LANES
        high, mid, low = split3(whole)
        left = jnp.concatenate([p[:, base:] for p in (high, high, mid, high, low, mid)], axis=0)
        right = jnp.concatenate([high, mid, high, low, high, mid], axis=0)
        update = lax.dot_general(left, right, (((0,), (0,)), ((), ())), preferred_element_type=jnp.float32)
        old = jnp.where((lane_wide >= end - BLOCK) & (lane_wide < end), 0.0, work[end:, :])
        work[end:, :] = old - update[end - base :, :]
    return jnp.sum(jnp.log(pivots)) / TILE


def send_kernel(panel_index, features, factor_prev, send):
    fac = factor_prev[...].astype(jnp.float32).reshape(CHUNKS, PIECE, LANES)
    feat = features[...].astype(jnp.float32).reshape(CHUNKS, PIECE, LANES)
    send[...] = jnp.concatenate([fac, feat], axis=1).astype(jnp.bfloat16)


def factor_kernel(where, my_feat, panel_fac, panel_feat, inverse, log_det, kernel, work):
    row = lax.broadcasted_iota(jnp.int32, (TILE, TILE), 0)
    col = lax.broadcasted_iota(jnp.int32, (TILE, TILE), 1)
    feat = panel_feat[...]
    fac = panel_fac[...]
    work[...] = tile_kernel(feat, feat, row == col) - dot_last(fac, fac)
    log_det[...] = jnp.full((1, LANES), factor_tile(work, inverse), jnp.float32)
    kernel[...] = tile_kernel(my_feat[...], feat, (row == col) & (where[1] == where[2]))


def panel_kernel(where, fac, panel_fac, kernel, inverse, panel):
    rows = jnp.concatenate([fac[z] for z in range(fac.shape[0])], axis=1)
    block = kernel[...] - dot_last(rows, panel_fac[...])
    result = lax.dot_general(
        block,
        inverse[...],
        (((1,), (1,)), ((), ())),
        precision=lax.Precision.HIGHEST,
        preferred_element_type=jnp.float32,
    )
    panel[...] = jnp.where(where[1] >= where[2], result, 0.0)


def groups_of(axis):
    index = np.arange(32).reshape(4, 4, 2)
    return np.moveaxis(index, {"y": 0, "x": 1}[axis], 2).reshape(-1, 4).tolist()


def gather_panel(send, owner_row):
    width = send.shape[2]
    col_count = lax.axis_size("col")
    got = lax.all_to_all(send, "row", 0, 0, tiled=True)
    slot = lax.dynamic_index_in_dim(got, owner_row, 0, keepdims=False)
    copies = jnp.broadcast_to(slot[None, :PIECE], (col_count, PIECE, width))
    layers = lax.all_to_all(copies, "col", 0, 0, tiled=True)
    return layers, slot[PIECE:]


def gather_chunks(layers, feat):
    col_count, _, width = layers.shape
    chunk = jnp.concatenate([layers.reshape(col_count * PIECE, width), feat], axis=0)
    over_x = lax.all_gather(chunk, "row", axis=0, axis_index_groups=groups_of("x"))
    mine = lax.all_gather(over_x, "row", axis=0, axis_index_groups=groups_of("y"))
    other = lax.ppermute(mine, "row", [(i, i ^ 1) for i in range(32)])
    first = lax.axis_index("row") % 2 == 0
    both = jnp.stack([jnp.where(first, mine, other), jnp.where(first, other, mine)], axis=2)
    fac = both[:, :, :, : col_count * PIECE].reshape(CHUNKS, col_count, PIECE, width)
    fac = fac.transpose(0, 2, 1, 3).reshape(TILE, col_count * width)
    return fac, both[:, :, :, col_count * PIECE :].reshape(TILE, width)


def body(features, factor_prev, panel_index):
    row_count = lax.axis_size("row")
    col_count = lax.axis_size("col")
    my_rows = features.shape[0] // col_count
    width = factor_prev.shape[1]
    panel_tile = panel_index[0]
    owner_row = panel_tile % row_count
    my_col = lax.axis_index("col")
    my_row = lax.axis_index("row")
    tiles = factor_prev.reshape(col_count, my_rows, width)
    tile_rows = pl.BlockSpec((TILE, LANES), lambda i, index: (lax.div(index[0], row_count), 0))
    send = pl.pallas_call(
        send_kernel,
        out_shape=jax.ShapeDtypeStruct((CHUNKS, 2 * PIECE, LANES), jnp.bfloat16),
        grid_spec=pltpu.PrefetchScalarGridSpec(
            num_scalar_prefetch=1,
            grid=(1,),
            in_specs=[tile_rows, tile_rows],
            out_specs=pl.BlockSpec((CHUNKS, 2 * PIECE, LANES), lambda i, index: (0, 0, 0)),
        ),
    )(panel_index, features, factor_prev)
    layers, feat_rows = gather_panel(send, owner_row)
    tiles, layers = lax.optimization_barrier((tiles, layers))
    my_fac = lax.all_to_all(tiles, "col", 0, 0, tiled=True)
    panel_fac, panel_feat = gather_chunks(layers, feat_rows)
    tile_of = my_col * row_count + my_row
    where = jnp.stack([my_col, tile_of, panel_tile]).astype(jnp.int32)
    whole = lambda *shape: pl.BlockSpec(shape, lambda i, where: (0,) * len(shape))
    inverse, log_det, kernel = pl.pallas_call(
        factor_kernel,
        out_shape=(
            jax.ShapeDtypeStruct((TILE, TILE), jnp.float32),
            jax.ShapeDtypeStruct((1, LANES), jnp.float32),
            jax.ShapeDtypeStruct((TILE, TILE), jnp.float32),
        ),
        grid_spec=pltpu.PrefetchScalarGridSpec(
            num_scalar_prefetch=1,
            grid=(1,),
            in_specs=[
                pl.BlockSpec((TILE, FEAT), lambda i, where: (where[0], 0)),
                whole(TILE, col_count * width),
                whole(TILE, FEAT),
            ],
            out_specs=(whole(TILE, TILE), whole(1, LANES), whole(TILE, TILE)),
            scratch_shapes=[pltpu.VMEM((TILE, TILE), jnp.float32)],
        ),
        compiler_params=pltpu.CompilerParams(vmem_limit_bytes=VMEM_LIMIT),
        cost_estimate=pl.CostEstimate(flops=10**10, bytes_accessed=4 * 10**6, transcendentals=10**5),
    )(where, features, panel_fac, panel_feat)
    vmem = pl.BlockSpec(memory_space=pltpu.VMEM)
    panel = pl.pallas_call(
        panel_kernel,
        out_shape=jax.ShapeDtypeStruct((TILE, TILE), jnp.float32),
        in_specs=[pl.BlockSpec(memory_space=pltpu.SMEM), vmem, vmem, vmem, vmem],
        out_specs=vmem,
        compiler_params=pltpu.CompilerParams(vmem_limit_bytes=VMEM_LIMIT),
        cost_estimate=pl.CostEstimate(flops=10**9, bytes_accessed=4 * 10**6, transcendentals=10**5),
    )(where, my_fac, panel_fac, kernel, inverse)
    return (panel, log_det[0, :1])


def solution(mesh):
    in_specs = (P("row", None), P("row", "col"), P())
    out_specs = (P(("row", "col"), None), P())
    return jax.shard_map(body, mesh=mesh, in_specs=in_specs, out_specs=out_specs, check_vma=False)
```

```python
import jax
import jax.numpy as jnp
import numpy as np
from jax import lax
from jax.experimental import pallas as pl
from jax.experimental.pallas import tpu as pltpu
from jax.sharding import PartitionSpec as P

TILE = 256
FEAT = 128
NUGGET = 4.0
RANGE = 8.0
CHUNKS = 8
PIECE = TILE // CHUNKS
BLOCK = 32
SUB = 8
LANES = 128
VMEM_LIMIT = 40 * 2**20


def tile_kernel(row_feat, panel_feat, self_pair):
    row_wide = row_feat.astype(jnp.float32)
    panel_wide = panel_feat.astype(jnp.float32)
    row_square = jnp.sum(row_wide * row_wide, axis=1, keepdims=True)
    square = panel_wide * panel_wide
    high = square.astype(jnp.bfloat16)
    low = (square - high.astype(jnp.float32)).astype(jnp.bfloat16)
    ones = jnp.ones((SUB, panel_feat.shape[1]), jnp.bfloat16)
    panel_square = (dot_last(ones, high) + dot_last(ones, low))[:1, :]
    cross_term = dot_last(row_feat, panel_feat)
    squared = jnp.maximum(row_square + panel_square - 2.0 * cross_term, 0.0)
    distance = jnp.where(self_pair, 0.0, jnp.sqrt(squared))
    return jnp.exp(-distance / RANGE) + jnp.where(self_pair, NUGGET, 0.0)


def dot_last(a, b):
    return lax.dot_general(a, b, (((1,), (1,)), ((), ())), preferred_element_type=jnp.float32)


def split3(a):
    high = a.astype(jnp.bfloat16)
    rest = a - high.astype(jnp.float32)
    mid = rest.astype(jnp.bfloat16)
    low = (rest - mid.astype(jnp.float32)).astype(jnp.bfloat16)
    return high, mid, low


def factor_rows(work, inverse, block, pivots, sub, lane, lane_wide):
    count = BLOCK // SUB
    begin = block * BLOCK
    base = begin // LANES * LANES
    diag, rows = [], []
    for i in range(count):
        row = work[begin + i * SUB : begin + (i + 1) * SUB, :]
        diag.append(row[:, base : base + LANES])
        inside = (lane_wide >= begin) & (lane_wide < begin + BLOCK)
        eye = lane_wide == begin + i * SUB + lax.broadcasted_iota(jnp.int32, (SUB, TILE), 0)
        rows.append(jnp.where(inside, eye.astype(jnp.float32), row))

    def columns_of(j):
        first = begin - base + j * SUB
        return [
            [jnp.broadcast_to(diag[i][:, first + k : first + k + 1], (SUB, LANES)) for k in range(SUB)]
            for i in range(j, count)
        ]

    column = columns_of(0)
    for j in range(count):
        after = columns_of(j + 1) if j + 1 < count else []
        pivot = jnp.ones((SUB, LANES), jnp.float32)
        for k in range(SUB):
            value = jnp.broadcast_to(column[0][k][k : k + 1, :], (SUB, LANES))
            recip = 1.0 / value
            pivot = jnp.where(sub == k, value, pivot)
            factor = [c[k] * recip for c in column]
            factor[0] = jnp.where(sub > k, factor[0], 0.0)
            for m in range(k + 1, SUB):
                other = jnp.broadcast_to(column[0][k][m : m + 1, :], (SUB, LANES))
                for i in range(len(column)):
                    column[i][m] = column[i][m] - factor[i] * other
            for m in range(SUB if after else 0):
                other = jnp.broadcast_to(column[1][k][m : m + 1, :], (SUB, LANES))
                for i in range(len(after)):
                    after[i][m] = after[i][m] - factor[i + 1] * other
            row_k = jnp.broadcast_to(rows[j][k : k + 1, :], (SUB, TILE))
            diag_k = jnp.broadcast_to(diag[j][k : k + 1, :], (SUB, LANES))
            for i in range(len(column)):
                rows[j + i] = rows[j + i] - jnp.concatenate([factor[i], factor[i]], axis=1) * row_k
                diag[j + i] = diag[j + i] - factor[i] * diag_k
        scale = 1.0 / jnp.sqrt(pivot)
        pivots = jnp.where(lane == block * count + j, pivot, pivots)
        rows[j] = rows[j] * jnp.concatenate([scale, scale], axis=1)
        column = after
    whole = jnp.concatenate(rows, axis=0)
    inverse[begin : begin + BLOCK, :] = jnp.where(lane_wide < begin + BLOCK, whole, 0.0)
    return whole, pivots


def factor_tile(work, inverse):
    sub = lax.broadcasted_iota(jnp.int32, (SUB, LANES), 0)
    lane = lax.broadcasted_iota(jnp.int32, (SUB, LANES), 1)
    lane_wide = lax.broadcasted_iota(jnp.int32, (1, TILE), 1)
    pivots = jnp.ones((SUB, LANES), jnp.float32)
    for block in range(TILE // BLOCK):
        whole, pivots = factor_rows(work, inverse, block, pivots, sub, lane, lane_wide)
        end = (block + 1) * BLOCK
        if end == TILE:
            break
        base = end // LANES * LANES
        high, mid, low = split3(whole)
        left = jnp.concatenate([p[:, base:] for p in (high, high, mid, high, low, mid)], axis=0)
        right = jnp.concatenate([high, mid, high, low, high, mid], axis=0)
        update = lax.dot_general(left, right, (((0,), (0,)), ((), ())), preferred_element_type=jnp.float32)
        old = jnp.where((lane_wide >= end - BLOCK) & (lane_wide < end), 0.0, work[end:, :])
        work[end:, :] = old - update[end - base :, :]
    return jnp.sum(jnp.log(pivots)) / TILE


def send_kernel(panel_index, features, factor_prev, send):
    fac = factor_prev[...].astype(jnp.float32).reshape(CHUNKS, PIECE, LANES)
    feat = features[...].astype(jnp.float32).reshape(CHUNKS, PIECE, LANES)
    send[...] = jnp.concatenate([fac, feat], axis=1).astype(jnp.bfloat16)


def factor_kernel(where, my_feat, panel_fac, panel_feat, inverse, log_det, kernel, work):
    row = lax.broadcasted_iota(jnp.int32, (TILE, TILE), 0)
    col = lax.broadcasted_iota(jnp.int32, (TILE, TILE), 1)
    feat = panel_feat[...]
    fac = panel_fac[...]
    work[...] = tile_kernel(feat, feat, row == col) - dot_last(fac, fac)
    log_det[...] = jnp.full((1, LANES), factor_tile(work, inverse), jnp.float32)
    kernel[...] = tile_kernel(my_feat[...], feat, (row == col) & (where[1] == where[2]))


def panel_kernel(where, fac, panel_fac, kernel, inverse, panel):
    rows = jnp.concatenate([fac[z] for z in range(fac.shape[0])], axis=1)
    block = kernel[...] - dot_last(rows, panel_fac[...])
    result = lax.dot_general(
        block,
        inverse[...],
        (((1,), (1,)), ((), ())),
        precision=lax.Precision.HIGHEST,
        preferred_element_type=jnp.float32,
    )
    panel[...] = jnp.where(where[1] >= where[2], result, 0.0)


def groups_of(*axes):
    index = np.arange(32).reshape(4, 4, 2)
    place = [("y", "x", "core").index(axis) for axis in axes]
    size = int(np.prod([index.shape[p] for p in place]))
    return np.moveaxis(index, place, range(3 - len(place), 3)).reshape(-1, size).tolist()


def gather_panel(send, owner_row):
    width = send.shape[2]
    col_count = lax.axis_size("col")
    got = lax.all_to_all(send, "row", 0, 0, tiled=True, axis_index_groups=groups_of("x", "core"))
    slot = lax.dynamic_index_in_dim(got, owner_row % CHUNKS, 0, keepdims=False)
    copies = jnp.broadcast_to(slot[None, :PIECE], (col_count, PIECE, width))
    layers = lax.all_to_all(copies, "col", 0, 0, tiled=True)
    return layers, slot[PIECE:]


def gather_chunks(layers, feat, owner_row):
    col_count, _, width = layers.shape
    chunk = jnp.concatenate([layers.reshape(col_count * PIECE, width), feat], axis=0)
    over_y = lax.all_gather(chunk, "row", axis=0, axis_index_groups=groups_of("y"))
    chunk = lax.dynamic_index_in_dim(over_y, owner_row // CHUNKS, 0, keepdims=False)
    mine = lax.all_gather(chunk, "row", axis=0, axis_index_groups=groups_of("x"))
    other = lax.ppermute(mine, "row", [(i, i ^ 1) for i in range(32)])
    first = lax.axis_index("row") % 2 == 0
    both = jnp.stack([jnp.where(first, mine, other), jnp.where(first, other, mine)], axis=1)
    fac = both[:, :, : col_count * PIECE].reshape(CHUNKS, col_count, PIECE, width)
    fac = fac.transpose(0, 2, 1, 3).reshape(TILE, col_count * width)
    return fac, both[:, :, col_count * PIECE :].reshape(TILE, width)


def body(features, factor_prev, panel_index):
    row_count = lax.axis_size("row")
    col_count = lax.axis_size("col")
    my_rows = features.shape[0] // col_count
    width = factor_prev.shape[1]
    panel_tile = panel_index[0]
    owner_row = panel_tile % row_count
    my_col = lax.axis_index("col")
    my_row = lax.axis_index("row")
    tiles = factor_prev.reshape(col_count, my_rows, width)
    tile_rows = pl.BlockSpec((TILE, LANES), lambda i, index: (lax.div(index[0], row_count), 0))
    send = pl.pallas_call(
        send_kernel,
        out_shape=jax.ShapeDtypeStruct((CHUNKS, 2 * PIECE, LANES), jnp.bfloat16),
        grid_spec=pltpu.PrefetchScalarGridSpec(
            num_scalar_prefetch=1,
            grid=(1,),
            in_specs=[tile_rows, tile_rows],
            out_specs=pl.BlockSpec((CHUNKS, 2 * PIECE, LANES), lambda i, index: (0, 0, 0)),
        ),
    )(panel_index, features, factor_prev)
    layers, feat_rows = gather_panel(send, owner_row)
    tiles, layers = lax.optimization_barrier((tiles, layers))
    my_fac = lax.all_to_all(tiles, "col", 0, 0, tiled=True)
    panel_fac, panel_feat = gather_chunks(layers, feat_rows, owner_row)
    tile_of = my_col * row_count + my_row
    where = jnp.stack([my_col, tile_of, panel_tile]).astype(jnp.int32)
    whole = lambda *shape: pl.BlockSpec(shape, lambda i, where: (0,) * len(shape))
    inverse, log_det, kernel = pl.pallas_call(
        factor_kernel,
        out_shape=(
            jax.ShapeDtypeStruct((TILE, TILE), jnp.float32),
            jax.ShapeDtypeStruct((1, LANES), jnp.float32),
            jax.ShapeDtypeStruct((TILE, TILE), jnp.float32),
        ),
        grid_spec=pltpu.PrefetchScalarGridSpec(
            num_scalar_prefetch=1,
            grid=(1,),
            in_specs=[
                pl.BlockSpec((TILE, FEAT), lambda i, where: (where[0], 0)),
                whole(TILE, col_count * width),
                whole(TILE, FEAT),
            ],
            out_specs=(whole(TILE, TILE), whole(1, LANES), whole(TILE, TILE)),
            scratch_shapes=[pltpu.VMEM((TILE, TILE), jnp.float32)],
        ),
        compiler_params=pltpu.CompilerParams(vmem_limit_bytes=VMEM_LIMIT),
        cost_estimate=pl.CostEstimate(flops=10**10, bytes_accessed=4 * 10**6, transcendentals=10**5),
    )(where, features, panel_fac, panel_feat)
    vmem = pl.BlockSpec(memory_space=pltpu.VMEM)
    panel = pl.pallas_call(
        panel_kernel,
        out_shape=jax.ShapeDtypeStruct((TILE, TILE), jnp.float32),
        in_specs=[pl.BlockSpec(memory_space=pltpu.SMEM), vmem, vmem, vmem, vmem],
        out_specs=vmem,
        compiler_params=pltpu.CompilerParams(vmem_limit_bytes=VMEM_LIMIT),
        cost_estimate=pl.CostEstimate(flops=10**9, bytes_accessed=4 * 10**6, transcendentals=10**5),
    )(where, my_fac, panel_fac, kernel, inverse)
    return (panel, log_det[0, :1])


def solution(mesh):
    in_specs = (P("row", None), P("row", "col"), P())
    out_specs = (P(("row", "col"), None), P())
    return jax.shard_map(body, mesh=mesh, in_specs=in_specs, out_specs=out_specs, check_vma=False)
```

```python
import jax
import jax.numpy as jnp
import numpy as np
from jax import lax
from jax.experimental import pallas as pl
from jax.experimental.pallas import tpu as pltpu
from jax.sharding import PartitionSpec as P

TILE = 256
FEAT = 128
NUGGET = 4.0
RANGE = 8.0
CHUNKS = 8
PIECE = TILE // CHUNKS
BLOCK = 32
SUB = 8
LANES = 128
VMEM_LIMIT = 16 * 2**20


def tile_kernel(row_feat, panel_feat, self_pair):
    row_wide = row_feat.astype(jnp.float32)
    panel_wide = panel_feat.astype(jnp.float32)
    row_square = jnp.sum(row_wide * row_wide, axis=1, keepdims=True)
    square = panel_wide * panel_wide
    high = square.astype(jnp.bfloat16)
    low = (square - high.astype(jnp.float32)).astype(jnp.bfloat16)
    ones = jnp.ones((SUB, panel_feat.shape[1]), jnp.bfloat16)
    panel_square = (dot_last(ones, high) + dot_last(ones, low))[:1, :]
    cross_term = dot_last(row_feat, panel_feat)
    squared = jnp.maximum(row_square + panel_square - 2.0 * cross_term, 0.0)
    distance = jnp.where(self_pair, 0.0, jnp.sqrt(squared))
    return jnp.exp(-distance / RANGE) + jnp.where(self_pair, NUGGET, 0.0)


def dot_last(a, b):
    return lax.dot_general(a, b, (((1,), (1,)), ((), ())), preferred_element_type=jnp.float32)


def split3(a):
    high = a.astype(jnp.bfloat16)
    rest = a - high.astype(jnp.float32)
    mid = rest.astype(jnp.bfloat16)
    low = (rest - mid.astype(jnp.float32)).astype(jnp.bfloat16)
    return high, mid, low


def factor_rows(work, inverse, block, pivots, sub, lane, lane_wide):
    count = BLOCK // SUB
    begin = block * BLOCK
    base = begin // LANES * LANES
    diag, rows = [], []
    for i in range(count):
        row = work[begin + i * SUB : begin + (i + 1) * SUB, :]
        diag.append(row[:, base : base + LANES])
        inside = (lane_wide >= begin) & (lane_wide < begin + BLOCK)
        eye = lane_wide == begin + i * SUB + lax.broadcasted_iota(jnp.int32, (SUB, TILE), 0)
        rows.append(jnp.where(inside, eye.astype(jnp.float32), row))

    def columns_of(j):
        first = begin - base + j * SUB
        return [
            [jnp.broadcast_to(diag[i][:, first + k : first + k + 1], (SUB, LANES)) for k in range(SUB)]
            for i in range(j, count)
        ]

    column = columns_of(0)
    for j in range(count):
        after = columns_of(j + 1) if j + 1 < count else []
        pivot = jnp.ones((SUB, LANES), jnp.float32)
        for k in range(SUB):
            value = jnp.broadcast_to(column[0][k][k : k + 1, :], (SUB, LANES))
            recip = 1.0 / value
            pivot = jnp.where(sub == k, value, pivot)
            factor = [c[k] * recip for c in column]
            factor[0] = jnp.where(sub > k, factor[0], 0.0)
            for m in range(k + 1, SUB):
                other = jnp.broadcast_to(column[0][k][m : m + 1, :], (SUB, LANES))
                for i in range(len(column)):
                    column[i][m] = column[i][m] - factor[i] * other
            for m in range(SUB if after else 0):
                other = jnp.broadcast_to(column[1][k][m : m + 1, :], (SUB, LANES))
                for i in range(len(after)):
                    after[i][m] = after[i][m] - factor[i + 1] * other
            row_k = jnp.broadcast_to(rows[j][k : k + 1, :], (SUB, TILE))
            diag_k = jnp.broadcast_to(diag[j][k : k + 1, :], (SUB, LANES))
            for i in range(len(column)):
                rows[j + i] = rows[j + i] - jnp.concatenate([factor[i], factor[i]], axis=1) * row_k
                diag[j + i] = diag[j + i] - factor[i] * diag_k
        scale = 1.0 / jnp.sqrt(pivot)
        pivots = jnp.where(lane == block * count + j, pivot, pivots)
        rows[j] = rows[j] * jnp.concatenate([scale, scale], axis=1)
        column = after
    whole = jnp.concatenate(rows, axis=0)
    inverse[begin : begin + BLOCK, :] = jnp.where(lane_wide < begin + BLOCK, whole, 0.0)
    return whole, pivots


def factor_tile(work, inverse):
    sub = lax.broadcasted_iota(jnp.int32, (SUB, LANES), 0)
    lane = lax.broadcasted_iota(jnp.int32, (SUB, LANES), 1)
    lane_wide = lax.broadcasted_iota(jnp.int32, (1, TILE), 1)
    pivots = jnp.ones((SUB, LANES), jnp.float32)
    for block in range(TILE // BLOCK):
        whole, pivots = factor_rows(work, inverse, block, pivots, sub, lane, lane_wide)
        end = (block + 1) * BLOCK
        if end == TILE:
            break
        base = end // LANES * LANES
        high, mid, low = split3(whole)
        left = jnp.concatenate([p[:, base:] for p in (high, high, mid, high, low, mid)], axis=0)
        right = jnp.concatenate([high, mid, high, low, high, mid], axis=0)
        update = lax.dot_general(left, right, (((0,), (0,)), ((), ())), preferred_element_type=jnp.float32)
        old = jnp.where((lane_wide >= end - BLOCK) & (lane_wide < end), 0.0, work[end:, :])
        work[end:, :] = old - update[end - base :, :]
    return jnp.sum(jnp.log(pivots)) / TILE


def send_kernel(panel_index, factor_prev, send):
    send[...] = factor_prev[...].reshape(CHUNKS, PIECE, LANES)


def factor_kernel(panel_fac, panel_feat, inverse, log_det, work):
    row = lax.broadcasted_iota(jnp.int32, (TILE, TILE), 0)
    col = lax.broadcasted_iota(jnp.int32, (TILE, TILE), 1)
    feat = panel_feat[...]
    fac = panel_fac[...]
    work[...] = tile_kernel(feat, feat, row == col) - dot_last(fac, fac)
    log_det[...] = jnp.full((1, LANES), factor_tile(work, inverse), jnp.float32)


def panel_kernel(where, fac, panel_fac, feat, panel_feat, inverse, panel):
    row = lax.broadcasted_iota(jnp.int32, (TILE, TILE), 0)
    col = lax.broadcasted_iota(jnp.int32, (TILE, TILE), 1)
    kernel = tile_kernel(feat[...], panel_feat[...], (row == col) & (where[0] == where[1]))
    rows = jnp.concatenate([fac[z] for z in range(fac.shape[0])], axis=1)
    block = kernel - dot_last(rows, panel_fac[...])
    result = lax.dot_general(
        block,
        inverse[...],
        (((1,), (1,)), ((), ())),
        precision=lax.Precision.HIGHEST,
        preferred_element_type=jnp.float32,
    )
    panel[...] = jnp.where(where[0] >= where[1], result, 0.0)


def groups_of(*axes):
    index = np.arange(32).reshape(4, 4, 2)
    place = [("y", "x", "core").index(axis) for axis in axes]
    size = int(np.prod([index.shape[p] for p in place]))
    return np.moveaxis(index, place, range(3 - len(place), 3)).reshape(-1, size).tolist()


def gather_panel(send, owner_row):
    width = send.shape[2]
    col_count = lax.axis_size("col")
    got = lax.all_to_all(send, "row", 0, 0, tiled=True, axis_index_groups=groups_of("x", "core"))
    slot = lax.dynamic_index_in_dim(got, owner_row % CHUNKS, 0, keepdims=True)
    copies = jnp.broadcast_to(slot, (col_count, PIECE, width))
    return lax.all_to_all(copies, "col", 0, 0, tiled=True)


def gather_chunks(layers, own_feat, owner_row):
    col_count, _, width = layers.shape
    rows = col_count * PIECE
    chunk = jnp.concatenate([layers.reshape(rows, width), own_feat], axis=0)
    over_y = lax.all_gather(chunk, "row", axis=0, axis_index_groups=groups_of("y"))
    chunk = lax.dynamic_index_in_dim(over_y, owner_row // CHUNKS, 0, keepdims=False)
    mine = lax.all_gather(chunk, "row", axis=0, axis_index_groups=groups_of("x"))
    other = lax.ppermute(mine, "row", [(i, i ^ 1) for i in range(32)])
    first = lax.axis_index("row") % 2 == 0
    both = jnp.stack([jnp.where(first, mine, other), jnp.where(first, other, mine)], axis=1)
    both = both.reshape(CHUNKS, rows + TILE, width)
    fac = both[:, :rows].reshape(CHUNKS, col_count, PIECE, width)
    fac = fac.transpose(0, 2, 1, 3).reshape(TILE, col_count * width)
    return fac, lax.dynamic_index_in_dim(both, owner_row % CHUNKS, 0, keepdims=False)[rows:]


def body(features, factor_prev, panel_index):
    row_count = lax.axis_size("row")
    col_count = lax.axis_size("col")
    my_rows = features.shape[0] // col_count
    width = factor_prev.shape[1]
    panel_tile = panel_index[0]
    owner_row = panel_tile % row_count
    my_col = lax.axis_index("col")
    my_row = lax.axis_index("row")
    tiles = factor_prev.reshape(col_count, my_rows, width)
    send = pl.pallas_call(
        send_kernel,
        out_shape=jax.ShapeDtypeStruct((CHUNKS, PIECE, LANES), jnp.bfloat16),
        grid_spec=pltpu.PrefetchScalarGridSpec(
            num_scalar_prefetch=1,
            grid=(1,),
            in_specs=[pl.BlockSpec((TILE, LANES), lambda i, index: (lax.div(index[0], row_count), 0))],
            out_specs=pl.BlockSpec((CHUNKS, PIECE, LANES), lambda i, index: (0, 0, 0)),
        ),
    )(panel_index, factor_prev)
    layers = gather_panel(send, owner_row)
    tiles, features, layers = lax.optimization_barrier((tiles, features, layers))
    my_fac = lax.all_to_all(tiles, "col", 0, 0, tiled=True)
    own_feat = lax.dynamic_slice_in_dim(features, panel_tile // row_count * TILE, TILE, 0)
    panel_fac, panel_feat = gather_chunks(layers, own_feat, owner_row)
    my_feat = lax.dynamic_slice_in_dim(features, my_col * my_rows, my_rows, 0)
    vmem = pl.BlockSpec(memory_space=pltpu.VMEM)
    inverse, log_det = pl.pallas_call(
        factor_kernel,
        out_shape=(
            jax.ShapeDtypeStruct((TILE, TILE), jnp.float32),
            jax.ShapeDtypeStruct((1, LANES), jnp.float32),
        ),
        in_specs=[vmem, vmem],
        out_specs=(vmem, vmem),
        scratch_shapes=[pltpu.VMEM((TILE, TILE), jnp.float32)],
        compiler_params=pltpu.CompilerParams(vmem_limit_bytes=VMEM_LIMIT),
        cost_estimate=pl.CostEstimate(flops=8 * 10**9, bytes_accessed=4 * 10**6, transcendentals=10**5),
    )(panel_fac, panel_feat)
    tile_of = my_col * row_count + my_row
    where = jnp.stack([tile_of, panel_tile]).astype(jnp.int32)
    panel = pl.pallas_call(
        panel_kernel,
        out_shape=jax.ShapeDtypeStruct((TILE, TILE), jnp.float32),
        in_specs=[pl.BlockSpec(memory_space=pltpu.SMEM), vmem, vmem, vmem, vmem, vmem],
        out_specs=vmem,
        compiler_params=pltpu.CompilerParams(vmem_limit_bytes=VMEM_LIMIT),
        cost_estimate=pl.CostEstimate(flops=10**9, bytes_accessed=4 * 10**6, transcendentals=10**5),
    )(where, my_fac, panel_fac, my_feat, panel_feat, inverse)
    return (panel, log_det[0, :1])


def solution(mesh):
    in_specs = (P("row", None), P("row", "col"), P())
    out_specs = (P(("row", "col"), None), P())
    return jax.shard_map(body, mesh=mesh, in_specs=in_specs, out_specs=out_specs, check_vma=False)
```
